512 devices in a mesh: elem: 16 (over y, x_hi), pulse: 32 (over x_lo, z, core).
Axes of the slice: x: 4 (x_hi: 2, x_lo: 2; x = x_hi * 2 + x_lo), y: 8, z: 8, core: 2. Of those that a mesh axis runs over, the one named last changes fastest.
Arguments:
- echoes: bfloat16 [2, 2048, 256, 1024], P(None, 'elem', 'pulse'), may hold values from -6 to 6
- keep_mask: int32 [256, 32], P('pulse'), may hold values from 0 to 1, as said below
- steer_index: int32 [512], replicated, may hold values from 0 to 1023
- element_position: float32 [2048], replicated, may hold values from 0 to 1024
- element_gain: float32 [2, 2048], replicated, may hold values from -4 to 4
- steer_sines: float32 [1024], replicated, may hold values from -1 to 1
Outputs:
- doppler_power: float32 [512, 256, 1024], P('pulse', None, 'elem')
The draws below stay inside these ranges and needn't reach their ends.
Inputs may be any that keep to these rules, and one draw needn't show every extreme that they name: `keep_mask`: in each masking block, each aligned run of 8 pulses keeps at most 6 pulses, and at least one; in every masking block some run keeps exactly 6.
All inputs are finite; a program needn't handle non-finite values.
Results may differ from the reference program's by a relative error of at most 0.005.
Values may be sent and summed in bfloat16 or wider, within the bound.
A program may use at most 128 MiB of HBM per device.

```python
import math
import jax
import jax.numpy as jnp
from jax import lax

E = 2048
B = 512
P_SIZE = 256
NV = 1024
RBLK = 32
R = 1024
NRB = 32
PL = 8
KEPT = 6


def draw_keep_mask(key, part):
    count_key, top_key, order_key = jax.random.split(jax.random.fold_in(key, 7), 3)
    blocks = R // RBLK
    runs = P_SIZE // PL
    counts = jax.random.randint(count_key, (runs, blocks), max(1, PL // 4), KEPT + 1)
    top = jax.random.randint(top_key, (blocks,), 0, runs)
    counts = jnp.where(jnp.arange(runs, dtype=jnp.int32)[:, None] == top[None, :], KEPT, counts)
    order_keys = jax.random.split(order_key, runs * blocks)
    ranks = jax.vmap(lambda one: jax.random.permutation(one, PL))(order_keys)
    ranks = jnp.transpose(ranks.reshape(runs, blocks, PL), (0, 2, 1))
    kept = ranks < counts[:, None, :]
    return kept.reshape(P_SIZE, blocks).astype(jnp.int32)


def plant(result, rng, low, high):
    index_at = [jax.random.randint(jax.random.fold_in(rng, axis), (), 0, length) for axis, length in enumerate(result.shape)]
    main_axis = result.shape.index(max(result.shape))
    neighbour = index_at[:main_axis] + [(index_at[main_axis] + 1) % result.shape[main_axis]] + index_at[main_axis + 1:]
    return result.at[tuple(index_at)].set(low).at[tuple(neighbour)].set(high)


def block_levels(own_key, dims, cuts, least, high):
    gain, own = 1.0, jax.random.fold_in(own_key, 6)
    for position, shards_of in cuts:
        draws = jnp.exp(jax.random.uniform(jax.random.fold_in(own, position), (shards_of,), jnp.float32, least / len(cuts), high / len(cuts)))
        gain = gain * jnp.repeat(draws, dims[position] // shards_of).reshape([-1 if axis == position else 1 for axis in range(len(dims))])
    return gain


def noise(stream_key, dims, scale, limit, shards=(), held_as=jnp.bfloat16):
    gain = block_levels(stream_key, dims, shards, -0.22, 0.18) if shards else 1.0
    result = jax.random.normal(stream_key, dims, jnp.float32) * scale * gain
    return jnp.minimum(jnp.maximum(result, -limit), limit).astype(held_as)


def setup_inputs(seed: int = 0) -> dict:
    seeds = jax.random.split(jax.random.key(seed), 7)
    echoes = noise(seeds[0], (2, E, P_SIZE, R), 1.0, 6.0, ((1, 16), (2, 32)))
    keep_mask = draw_keep_mask(jax.random.fold_in(seeds[6], 71), 0)
    steer_index = plant(jax.random.randint(seeds[2], (B,), 0, NV), jax.random.fold_in(seeds[2], 1), 0, NV - 1).astype(jnp.int32)
    element_position = jnp.clip(jax.random.uniform(seeds[3], (E,), jnp.float32, 0.0, 1024.0), 0.0, 1024.0)
    element_gain = noise(seeds[4], (2, E), 1.0, 4.0, (), jnp.float32)
    steer_sines = jnp.clip(jax.random.uniform(seeds[5], (NV,), jnp.float32, -1.0, 1.0), -1.0, 1.0)
    return {"echoes": echoes, "keep_mask": keep_mask, "steer_index": steer_index, "element_position": element_position, "element_gain": element_gain, "steer_sines": steer_sines}


def steering(element_position, element_gain, sines):
    phase = 2.0 * math.pi * element_position[:, None] * sines[None, :]
    cosine = jnp.cos(phase)
    sine = jnp.sin(phase)
    factor = 1.0 / math.sqrt(E)
    real = (element_gain[0][:, None] * cosine + element_gain[1][:, None] * sine) * factor
    imag = (element_gain[1][:, None] * cosine - element_gain[0][:, None] * sine) * factor
    return (real.astype(jnp.bfloat16), imag.astype(jnp.bfloat16))

def tables(count):
    index = jnp.arange(count, dtype=jnp.int32)
    angle = 2.0 * math.pi * (index[:, None] * index[None, :] % count).astype(jnp.float32) / count
    taper = 0.54 - 0.46 * jnp.cos(2.0 * math.pi * index.astype(jnp.float32) / (count - 1))
    taper = taper / math.sqrt(count)
    cos_table = jnp.cos(angle) * taper[None, :]
    sin_table = jnp.sin(angle) * taper[None, :]
    upper = jnp.concatenate((cos_table, sin_table), axis=1)
    lower = jnp.concatenate((-sin_table, cos_table), axis=1)
    transform = jnp.concatenate((upper, lower), axis=0)
    high = transform.astype(jnp.bfloat16)
    low = (transform - high.astype(jnp.float32)).astype(jnp.bfloat16)
    return (high, low)

def contract(left, right):
    return lax.dot_general(left, right, (((0,), (0,)), ((), ())), preferred_element_type=jnp.float32)

def beamform(weight_re, weight_im, sample_re, sample_im):
    real = contract(weight_re, sample_re) - contract(weight_im, sample_im)
    imag = contract(weight_re, sample_im) + contract(weight_im, sample_re)
    return (real, imag)

def spectrum(high, low, beam_re, beam_im):
    count = beam_re.shape[1]
    total = jnp.zeros((beam_re.shape[0], 2 * count, beam_re.shape[2]), jnp.float32)
    for table in (high, low):
        left = table[:, :count].astype(jnp.float32)
        right = table[:, count:].astype(jnp.float32)
        total = total + jnp.einsum('fp,bpn->bfn', left, beam_re.astype(jnp.float32), precision=lax.Precision.HIGHEST)
        total = total + jnp.einsum('fp,bpn->bfn', right, beam_im.astype(jnp.float32), precision=lax.Precision.HIGHEST)
    real = total[:, :count]
    imag = total[:, count:]
    return real * real + imag * imag

def reference(echoes, keep_mask, steer_index, element_position, element_gain, steer_sines):
    sines = steer_sines[steer_index]
    weight_re, weight_im = steering(element_position, element_gain, sines)
    high, low = tables(P_SIZE)

    def block(index):
        start = (index * RBLK).astype(jnp.int32)
        piece = lax.dynamic_slice_in_dim(echoes, start, RBLK, 3)
        keeper = lax.dynamic_slice_in_dim(keep_mask, index.astype(jnp.int32), 1, 1)
        keeper = keeper.astype(jnp.bfloat16)[None, None, :, :]
        piece = piece * keeper
        flat = piece.reshape(2, E, P_SIZE * RBLK)
        real, imag = beamform(weight_re, weight_im, flat[0], flat[1])
        real = real.astype(jnp.bfloat16).reshape(B, P_SIZE, RBLK)
        imag = imag.astype(jnp.bfloat16).reshape(B, P_SIZE, RBLK)
        return spectrum(high, low, real, imag)
    stacked = lax.map(block, jnp.arange(NRB, dtype=jnp.int32))
    return jnp.transpose(stacked, (1, 2, 0, 3)).reshape(B, P_SIZE, NRB * RBLK)
```

```python
import math

import jax
import jax.numpy as jnp
from jax import lax
from jax.sharding import PartitionSpec as P

E = 2048
P_SIZE = 256
RBLK = 32


def steering(element_position, element_gain, sines):
    phase = 2.0 * math.pi * element_position[:, None] * sines[None, :]
    cosine = jnp.cos(phase)
    sine = jnp.sin(phase)
    factor = 1.0 / math.sqrt(E)
    real = (element_gain[0][:, None] * cosine + element_gain[1][:, None] * sine) * factor
    imag = (element_gain[1][:, None] * cosine - element_gain[0][:, None] * sine) * factor
    return (real.astype(jnp.bfloat16), imag.astype(jnp.bfloat16))


def tables(count):
    index = jnp.arange(count, dtype=jnp.int32)
    angle = 2.0 * math.pi * (index[:, None] * index[None, :] % count).astype(jnp.float32) / count
    taper = 0.54 - 0.46 * jnp.cos(2.0 * math.pi * index.astype(jnp.float32) / (count - 1))
    taper = taper / math.sqrt(count)
    cos_table = jnp.cos(angle) * taper[None, :]
    sin_table = jnp.sin(angle) * taper[None, :]
    upper = jnp.concatenate((cos_table, sin_table), axis=1)
    lower = jnp.concatenate((-sin_table, cos_table), axis=1)
    transform = jnp.concatenate((upper, lower), axis=0)
    high = transform.astype(jnp.bfloat16)
    low = (transform - high.astype(jnp.float32)).astype(jnp.bfloat16)
    return (high, low)


def contract(left, right):
    return lax.dot_general(
        left, right, (((0,), (0,)), ((), ())), preferred_element_type=jnp.float32
    )


def per_device(echoes, keep_mask, steer_index, element_position, element_gain, steer_sines):
    choices_all = jnp.arange(steer_sines.shape[0], dtype=jnp.int32)
    sines = jnp.sum(
        jnp.where(steer_index[:, None] == choices_all[None, :], steer_sines[None, :], 0.0), axis=1
    )
    weight_re, weight_im = steering(element_position, element_gain, sines)
    high, low = tables(P_SIZE)
    count = P_SIZE
    groups = lax.axis_size("elem")
    local_elems = echoes.shape[1]
    local_pulses = echoes.shape[2]
    total_cells = echoes.shape[3]
    cells = total_cells // groups
    blocks_all = keep_mask.shape[1]
    kept_slots = (3 * local_pulses + 3) // 4
    offset = lax.axis_index("elem") * cells
    pulse_ids = jnp.arange(local_pulses, dtype=jnp.int32)
    earlier = pulse_ids[None, :, None] <= pulse_ids[:, None, None]
    rank = jnp.sum(jnp.where(earlier, keep_mask[None, :, :], 0), axis=1) - 1
    slot_ids = jnp.arange(kept_slots, dtype=jnp.int32)
    selector = (
        (keep_mask[None, :, :] == 1) & (rank[None, :, :] == slot_ids[:, None, None])
    ).astype(jnp.bfloat16)
    shaped5 = echoes.reshape(2, local_elems, local_pulses, blocks_all, total_cells // blocks_all)
    prepared = jnp.einsum("spk,cepkr->ceskr", selector, shaped5, preferred_element_type=jnp.float32)
    prepared = prepared.astype(jnp.bfloat16).reshape(2, local_elems, kept_slots, total_cells)
    turned = lax.all_to_all(prepared, "elem", split_axis=3, concat_axis=1, tiled=True)
    span = turned.shape[3]
    flat = turned.reshape(2, turned.shape[1], turned.shape[2] * span)
    real = contract(weight_re, flat[0]) - contract(weight_im, flat[1])
    imag = contract(weight_re, flat[1]) + contract(weight_im, flat[0])
    real = real.astype(jnp.bfloat16).reshape(-1, turned.shape[2], span)
    imag = imag.astype(jnp.bfloat16).reshape(-1, turned.shape[2], span)
    packed_re = real
    packed_im = imag
    block_ids = jnp.arange(blocks_all, dtype=jnp.int32)
    onehot = (
        (offset + jnp.arange(cells, dtype=jnp.int32))[:, None] // RBLK == block_ids[None, :]
    ).astype(jnp.bfloat16)
    spread = jnp.einsum("spk,nk->spn", selector, onehot, preferred_element_type=jnp.float32).astype(
        jnp.bfloat16
    )
    real = jnp.einsum("spn,bsn->bpn", spread, packed_re, preferred_element_type=jnp.float32).astype(
        jnp.bfloat16
    )
    imag = jnp.einsum("spn,bsn->bpn", spread, packed_im, preferred_element_type=jnp.float32).astype(
        jnp.bfloat16
    )
    beam_re = lax.all_to_all(real, "pulse", split_axis=0, concat_axis=1, tiled=True)
    beam_im = lax.all_to_all(imag, "pulse", split_axis=0, concat_axis=1, tiled=True)
    total = None
    for table in (high, low):
        part_re = jnp.einsum(
            "fp,bpn->bfn", table[:, :count], beam_re, preferred_element_type=jnp.float32
        )
        part_im = jnp.einsum(
            "fp,bpn->bfn", table[:, count:], beam_im, preferred_element_type=jnp.float32
        )
        total = part_re + part_im if total is None else total + part_re + part_im
    doppler_real = total[:, :count]
    doppler_imag = total[:, count:]
    return doppler_real * doppler_real + doppler_imag * doppler_imag


def solution(mesh):
    placed = (P(None, "elem", "pulse", None), P("pulse", None), P(), P(), P(), P())
    return jax.shard_map(
        per_device, mesh=mesh, in_specs=placed, out_specs=P("pulse", None, "elem"), check_vma=False
    )
```

```python
import functools
import math

import jax
import jax.numpy as jnp
from jax import lax
from jax.experimental import pallas as pl
from jax.experimental.pallas import tpu as pltpu
from jax.sharding import PartitionSpec as P

F32 = jnp.float32
BF16 = jnp.bfloat16
I32 = jnp.int32
E = 2048
BEAMS = 512
PULSES = 256
CELLS = 1024
BLOCKS = 32
RUN = 8
SLOTS = 6
NE = 16
NP = 32
LE = E // NE
LB = BEAMS // NP
LC = CELLS // NE
CHUNKS = 3


def turn(t):
    a = t * math.pi
    q = a * a
    s = a * (1.0 + q * (-1 / 6 + q * (1 / 120 + q * (-1 / 5040 + q * (1 / 362880 - q / 39916800)))))
    c = 1.0 + q * (-1 / 2 + q * (1 / 24 + q * (-1 / 720 + q * (1 / 40320 + q * (-1 / 3628800 + q / 479001600)))))
    return 1.0 - 2.0 * s * s, 2.0 * s * c


def iota(shape, dim):
    return lax.broadcasted_iota(I32, shape, dim)


def slot_pulses(keep):
    count = jnp.zeros_like(keep[0:1])
    first = jnp.zeros_like(count)
    second = jnp.zeros_like(count)
    for p in range(RUN):
        count = count + (1.0 - keep[p : p + 1])
        first = first + jnp.where(count < 0.5, 1.0, 0.0)
        second = second + jnp.where(count < 1.5, 1.0, 0.0)
    return [
        s + jnp.where(first < s + 0.5, 1.0, 0.0) + jnp.where(second < s + 1.5, 1.0, 0.0)
        for s in range(SLOTS)
    ]


def kernel(
    x_ref, mask_ref, index_ref, pos_ref, gain_ref, sines_ref, out_ref,
    prep, xbuf, wr, wi, beams, ybuf, fbuf, mine, mbuf, coef, perm, tab, tsel, xt, column,
    msend, mrecv, xsend, xrecv, bsend, brecv,
):
    em = lax.axis_index("elem")
    pm = lax.axis_index("pulse")
    barrier = pltpu.get_barrier_semaphore()

    def elem_peer(k):
        return lax.rem(em + k, NE)

    def pulse_peer(k):
        return lax.rem(pm + k, NP)

    def greet_elem(k, carry):
        pl.semaphore_signal(barrier, inc=1, device_id=(elem_peer(k), pm), device_id_type=pl.DeviceIdType.MESH)
        return carry

    def greet_pulse(k, carry):
        pl.semaphore_signal(barrier, inc=1, device_id=(em, pulse_peer(k)), device_id_type=pl.DeviceIdType.MESH)
        return carry

    lax.fori_loop(1, NE, greet_elem, 0)
    lax.fori_loop(1, NP, greet_pulse, 0)

    keep = mask_ref[...].astype(F32)
    blocks_of = iota((BLOCKS, CELLS), 1) // (CELLS // BLOCKS) == iota((BLOCKS, CELLS), 0)
    keep_cells = jnp.dot(keep, jnp.where(blocks_of, 1.0, 0.0), preferred_element_type=F32)
    pulses = slot_pulses(keep_cells)
    for s in range(SLOTS):
        for d in range(3):
            use = jnp.where(jnp.abs(pulses[s] - (s + d)) < 0.5, 1.0, 0.0)
            coef[3 * s + d : 3 * s + d + 1, :] = use * keep_cells[s + d : s + d + 1]
    narrow = jnp.where(iota((BLOCKS, 128), 1) == iota((BLOCKS, 128), 0), 1.0, 0.0)
    pulses = slot_pulses(jnp.dot(keep, narrow, preferred_element_type=F32))
    mine[...] = jnp.zeros_like(mine)
    for s in range(SLOTS):
        mine[s : s + 1, :] = pulses[s]
    mbuf[pl.ds(pl.multiple_of(pm * RUN, RUN), RUN), :] = mine[...]

    row, col = iota((256, 256), 0), iota((256, 256), 1)
    hit = (row // 32 == col % 8) & (row % 32 == col // 8)
    perm[...] = jnp.where(hit, 1.0, 0.0).astype(BF16)

    low_half = iota((32, 128), 1) < LC

    def pack(step, carry):
        pair = step // 8
        c = (step // 4) % 2
        group = step % 4
        lanes = pl.ds(pl.multiple_of(pair * 256, 256), 256)
        rows = pl.ds(pl.multiple_of(group * 256, 256), 256)
        turned = jnp.dot(perm[...], x_ref[c, rows, lanes], preferred_element_type=F32)
        parts = [turned[32 * p : 32 * p + 32] for p in range(RUN)]
        slots = []
        for s in range(SLOTS):
            total = parts[s] * coef[3 * s : 3 * s + 1, lanes]
            for d in (1, 2):
                total = total + parts[s + d] * coef[3 * s + d : 3 * s + d + 1, lanes]
            slots.append(total)
        for t in range(2):
            for j in range(CHUNKS):
                a = slots[j][:, 128 * t : 128 * t + 128]
                b = slots[j + 3][:, 128 * t : 128 * t + 128]
                first = jnp.where(low_half, a, pltpu.roll(b, LC, 1))
                second = jnp.where(low_half, pltpu.roll(a, LC, 1), b)
                at = pl.ds(pl.multiple_of(group * 32, 32), 32)
                to = pl.ds(pl.multiple_of(c * 128, 128), 128)
                prep[j, 4 * pair + 2 * t, at, to] = first.astype(BF16)
                prep[j, 4 * pair + 2 * t + 1, at, to] = second.astype(BF16)
        return carry

    lax.fori_loop(0, 32, pack, 0)

    pl.semaphore_wait(barrier, NE + NP - 2)

    my_rows = pl.ds(pl.multiple_of(em * LE, LE), LE)

    def send_samples(j):
        def one(k, carry):
            pltpu.make_async_remote_copy(
                src_ref=prep.at[j, elem_peer(k)],
                dst_ref=xbuf.at[j, my_rows],
                send_sem=xsend.at[j],
                recv_sem=xrecv.at[j],
                device_id=(elem_peer(k), pm),
                device_id_type=pl.DeviceIdType.MESH,
            ).start()
            return carry

        lax.fori_loop(1, NE, one, 0)

    def send_slots(k, carry):
        pltpu.make_async_remote_copy(
            src_ref=mine,
            dst_ref=mbuf.at[pl.ds(pl.multiple_of(pm * RUN, RUN), RUN)],
            send_sem=msend,
            recv_sem=mrecv,
            device_id=(em, pulse_peer(k)),
            device_id_type=pl.DeviceIdType.MESH,
        ).start()
        return carry

    send_samples(0)
    lax.fori_loop(1, NP, send_slots, 0)
    send_samples(1)
    send_samples(2)
    for j in range(CHUNKS):
        xbuf[j, my_rows, :] = prep[j, em]

    eye = iota((128, 128), 0) == iota((128, 128), 1)
    for i in range(BEAMS // 128):
        line = index_ref[0:1, 128 * i : 128 * i + 128].astype(F32)
        wanted = jnp.sum(jnp.where(eye, line, 0.0), axis=1, keepdims=True)
        choice = iota((128, sines_ref.shape[1]), 1).astype(F32) == wanted
        picked = jnp.sum(jnp.where(choice, sines_ref[...], 0.0), axis=1, keepdims=True)
        column[128 * i : 128 * i + 128, :] = jnp.broadcast_to(picked, (128, 128))

    factor = 1.0 / math.sqrt(E)

    def weigh(step, carry):
        rows = pl.ds(pl.multiple_of((step // 16) * 64, 64), 64)
        lanes = pl.ds(pl.multiple_of((step % 16) * 128, 128), 128)
        turns = pos_ref[0:1, lanes] * column[rows, :]
        cosine, sine = turn(turns - jnp.round(turns))
        real, imag = gain_ref[0:1, lanes] * factor, gain_ref[1:2, lanes] * factor
        wr[rows, lanes] = (real * cosine + imag * sine).astype(BF16)
        wi[rows, lanes] = (imag * cosine - real * sine).astype(BF16)
        return carry

    lax.fori_loop(0, 8 * 16, weigh, 0)

    def tabulate(step, carry):
        rows = pl.ds(pl.multiple_of(step * 32, 32), 32)
        p = iota((32, PULSES), 0) + step * 32
        product = jnp.bitwise_and(p * iota((32, PULSES), 1), PULSES - 1).astype(F32) / PULSES
        cosine, sine = turn(jnp.where(product < 0.5, product, product - 1.0))
        at = p.astype(F32) / (PULSES - 1)
        level, _ = turn(jnp.where(at < 0.5, at, at - 1.0))
        taper = (0.54 - 0.46 * level) / math.sqrt(PULSES)
        for i, value in enumerate((cosine * taper, sine * taper)):
            high = value.astype(BF16)
            tab[rows, 256 * i : 256 * i + 256] = high
            tab[rows, 512 + 256 * i : 512 + 256 * i + 256] = (value - high.astype(F32)).astype(BF16)
        return carry

    lax.fori_loop(0, PULSES // 32, tabulate, 0)

    def wait_bytes(ref, sem):
        pltpu.make_async_copy(ref, ref, sem).wait()

    wait_bytes(mbuf.at[pl.ds(0, RUN * (NP - 1))], mrecv)
    lane = iota((128, 128), 1)
    for k in range(2):
        for h in range(2):
            found = [mbuf[pl.ds(j + 3 * h, NP, stride=RUN), :] for j in range(CHUNKS)]
            found = jnp.concatenate(found + [jnp.zeros((NP, 128), F32)], axis=0)
            pulse = jnp.sum(jnp.where(lane == 2 * em + k, found, 0.0), axis=1, keepdims=True)
            row = iota((128, PULSES), 0)
            target = (RUN * (row % NP)).astype(F32) + pulse
            hit = (jnp.abs(iota((128, PULSES), 1).astype(F32) - target) < 0.5) & (row < 96)
            rows = jnp.dot(jnp.where(hit, 1.0, 0.0).astype(BF16), tab[...], preferred_element_type=F32)
            for part in range(2):
                cosine = rows[:, 512 * part : 512 * part + 256]
                sine = rows[:, 512 * part + 256 : 512 * part + 512]
                real = slice(128 * h, 128 * h + 128)
                imag = slice(256 + 128 * h, 256 + 128 * h + 128)
                tsel[k, part, real, 0:256] = cosine.astype(BF16)
                tsel[k, part, real, 256:512] = (-sine).astype(BF16)
                tsel[k, part, imag, 0:256] = sine.astype(BF16)
                tsel[k, part, imag, 256:512] = cosine.astype(BF16)

    my_beams = pl.ds(pl.multiple_of(pm * LB, LB), LB)
    for j in range(CHUNKS):
        wait_bytes(xbuf.at[j, pl.ds(0, LE * (NE - 1))], xrecv.at[j])

        def form(m, carry, j=j):
            rows = pl.ds(pl.multiple_of(m * 256, 256), 256)
            by_real = jnp.dot(wr[rows, :], xbuf[j], preferred_element_type=F32)
            by_imag = jnp.dot(wi[rows, :], xbuf[j], preferred_element_type=F32)
            beams[j, rows, 0:128] = (by_real[:, 0:128] - by_imag[:, 128:256]).astype(BF16)
            beams[j, rows, 128:256] = (by_real[:, 128:256] + by_imag[:, 0:128]).astype(BF16)
            return carry

        lax.fori_loop(0, 2, form, 0)

        def send_beams(k, carry, j=j):
            pltpu.make_async_remote_copy(
                src_ref=beams.at[j, pl.ds(pl.multiple_of(pulse_peer(k) * LB, LB), LB)],
                dst_ref=ybuf.at[j, my_beams],
                send_sem=bsend.at[j],
                recv_sem=brecv.at[j],
                device_id=(em, pulse_peer(k)),
                device_id_type=pl.DeviceIdType.MESH,
            ).start()
            return carry

        lax.fori_loop(1, NP, send_beams, 0)
        ybuf[j, my_beams, :] = beams[j, my_beams, :]

    for j in range(CHUNKS):
        wait_bytes(ybuf.at[j, pl.ds(0, LB * (NP - 1))], brecv.at[j])
        fbuf[0, 512 * j : 512 * j + 512, :] = ybuf[j, :, 0:128].astype(F32)
        fbuf[1, 512 * j : 512 * j + 512, :] = ybuf[j, :, 128:256].astype(F32)

    for b in range(LB):
        for c in range(2):
            got = [fbuf[c, pl.ds(512 * j + b, NP, stride=LB), :] for j in range(CHUNKS)]
            got = jnp.concatenate(got + [jnp.zeros((NP, 128), F32)], axis=0)
            flat = got.T.astype(BF16)
            for h in range(2):
                for k in range(2):
                    xt[k, 32 * b : 32 * b + 32, 256 * c + 128 * h : 256 * c + 128 * h + 128] = flat[
                        64 * h + 32 * k : 64 * h + 32 * k + 32
                    ]

    for k in range(2):
        for m in range(4):
            left = xt[k, 128 * m : 128 * m + 128, :]
            spec = jnp.dot(left, tsel[k, 0], preferred_element_type=F32)
            spec = spec + jnp.dot(left, tsel[k, 1], preferred_element_type=F32)
            power = spec[:, 0:256] * spec[:, 0:256] + spec[:, 256:512] * spec[:, 256:512]
            out_ref[4 * m : 4 * m + 4, 32 * k : 32 * k + 32, :] = power.reshape(4, 32, 256)

    wait_bytes(mbuf.at[pl.ds(0, RUN * (NP - 1))], msend)
    for j in range(CHUNKS):
        wait_bytes(xbuf.at[j, pl.ds(0, LE * (NE - 1))], xsend.at[j])
        wait_bytes(ybuf.at[j, pl.ds(0, LB * (NP - 1))], bsend.at[j])


def per_device(echoes, keep_mask, steer_index, element_position, element_gain, steer_sines):
    vmem = pl.BlockSpec(memory_space=pltpu.VMEM)
    dma = pltpu.SemaphoreType.DMA
    power = pl.pallas_call(
        kernel,
        out_shape=jax.ShapeDtypeStruct((LB, LC, PULSES), F32),
        in_specs=[vmem] * 6,
        out_specs=vmem,
        scratch_shapes=[
            pltpu.VMEM((CHUNKS, NE, LE, 256), BF16),
            pltpu.VMEM((CHUNKS, E, 256), BF16),
            pltpu.VMEM((BEAMS, E), BF16),
            pltpu.VMEM((BEAMS, E), BF16),
            pltpu.VMEM((CHUNKS, BEAMS, 256), BF16),
            pltpu.VMEM((CHUNKS, BEAMS, 256), BF16),
            pltpu.VMEM((2, CHUNKS * BEAMS, 128), F32),
            pltpu.VMEM((RUN, 128), F32),
            pltpu.VMEM((RUN * NP, 128), F32),
            pltpu.VMEM((3 * SLOTS, CELLS), F32),
            pltpu.VMEM((256, 256), BF16),
            pltpu.VMEM((PULSES, 1024), BF16),
            pltpu.VMEM((2, 2, 512, 512), BF16),
            pltpu.VMEM((2, 512, 512), BF16),
            pltpu.VMEM((BEAMS, 128), F32),
            dma, dma, dma((CHUNKS,)), dma((CHUNKS,)), dma((CHUNKS,)), dma((CHUNKS,)),
        ],
        compiler_params=pltpu.CompilerParams(
            collective_id=0, has_side_effects=True, vmem_limit_bytes=48 << 20
        ),
        name="integrate",
    )(
        echoes.reshape(2, LE * RUN, CELLS),
        keep_mask,
        steer_index.reshape(1, -1),
        element_position.reshape(1, -1),
        element_gain,
        steer_sines.reshape(1, -1),
    )
    return jnp.transpose(power, (0, 2, 1))


def solution(mesh):
    placed = (P(None, "elem", "pulse", None), P("pulse", None), P(), P(), P(), P())
    return jax.shard_map(
        per_device, mesh=mesh, in_specs=placed, out_specs=P("pulse", None, "elem"), check_vma=False
    )
```

```python
import functools
import math

import jax
import jax.numpy as jnp
from jax import lax
from jax.experimental import pallas as pl
from jax.experimental.pallas import tpu as pltpu
from jax.sharding import PartitionSpec as P

F32 = jnp.float32
BF16 = jnp.bfloat16
I32 = jnp.int32
E = 2048
BEAMS = 512
PULSES = 256
CELLS = 1024
BLOCKS = 32
RUN = 8
SLOTS = 6
NE = 16
NP = 32
LE = E // NE
LB = BEAMS // NP
LC = CELLS // NE
CHUNKS = 3
NY = 8
ORDER = (3, 5, 4, 2, 6, 1, 7, 0)


def turn(t):
    a = t * math.pi
    q = a * a
    s = a * (1.0 + q * (-1 / 6 + q * (1 / 120 + q * (-1 / 5040 + q * (1 / 362880 - q / 39916800)))))
    c = 1.0 + q * (-1 / 2 + q * (1 / 24 + q * (-1 / 720 + q * (1 / 40320 + q * (-1 / 3628800 + q / 479001600)))))
    return 1.0 - 2.0 * s * s, 2.0 * s * c


def iota(shape, dim):
    return lax.broadcasted_iota(I32, shape, dim)


def slot_pulses(keep):
    count = jnp.zeros_like(keep[0:1])
    first = jnp.zeros_like(count)
    second = jnp.zeros_like(count)
    for p in range(RUN):
        count = count + (1.0 - keep[p : p + 1])
        first = first + jnp.where(count < 0.5, 1.0, 0.0)
        second = second + jnp.where(count < 1.5, 1.0, 0.0)
    return [
        s + jnp.where(first < s + 0.5, 1.0, 0.0) + jnp.where(second < s + 1.5, 1.0, 0.0)
        for s in range(SLOTS)
    ]


def kernel(
    x_hbm, mask_hbm, index_hbm, pos_hbm, gain_hbm, sines_hbm, out_ref,
    x_ref, mask_ref, index_ref, pos_ref, gain_ref, sines_ref, prep, xbuf, wr, wi, beams, ybuf, fbuf, mine, mbuf, coef, perm, tab, tsel, xt, column,
    lsem, ssem, msend, mrecv, xsend, xrecv, bsend, brecv,
):
    em = lax.axis_index("elem")
    pm = lax.axis_index("pulse")
    barrier = pltpu.get_barrier_semaphore()

    small = [
        pltpu.make_async_copy(a, b, ssem.at[i])
        for i, (a, b) in enumerate((
            (mask_hbm, mask_ref), (index_hbm, index_ref), (pos_hbm, pos_ref), (gain_hbm, gain_ref), (sines_hbm, sines_ref)
        ))
    ]
    for copy in small:
        copy.start()

    def y_at(k):
        return lax.rem(em // 2 + k, NY)

    def y_lanes(k):
        return pl.ds(pl.multiple_of(y_at(k) * 128, 128), 128)

    def load(i):
        lanes = y_lanes(ORDER[i])
        return pltpu.make_async_copy(x_hbm.at[:, :, lanes], x_ref.at[:, :, lanes], lsem.at[i])

    for i in range(NY):
        load(i).start()
    def elem_peer(k):
        return lax.rem(em + k, NE)

    def pulse_peer(k):
        return lax.rem(pm + k, NP)

    def greet_elem(k, carry):
        pl.semaphore_signal(barrier, inc=1, device_id=(elem_peer(k), pm), device_id_type=pl.DeviceIdType.MESH)
        return carry

    def greet_pulse(k, carry):
        pl.semaphore_signal(barrier, inc=1, device_id=(em, pulse_peer(k)), device_id_type=pl.DeviceIdType.MESH)
        return carry

    lax.fori_loop(1, NE, greet_elem, 0)
    lax.fori_loop(1, NP, greet_pulse, 0)

    small[0].wait()
    keep = mask_ref[...].astype(F32)
    blocks_of = iota((BLOCKS, CELLS), 1) // (CELLS // BLOCKS) == iota((BLOCKS, CELLS), 0)
    keep_cells = jnp.dot(keep, jnp.where(blocks_of, 1.0, 0.0), preferred_element_type=F32)
    pulses = slot_pulses(keep_cells)
    for s in range(SLOTS):
        for d in range(3):
            use = jnp.where(jnp.abs(pulses[s] - (s + d)) < 0.5, 1.0, 0.0)
            coef[3 * s + d : 3 * s + d + 1, :] = use * keep_cells[s + d : s + d + 1]
    narrow = jnp.where(iota((BLOCKS, 128), 1) == iota((BLOCKS, 128), 0), 1.0, 0.0)
    pulses = slot_pulses(jnp.dot(keep, narrow, preferred_element_type=F32))
    mine[...] = jnp.zeros_like(mine)
    for s in range(SLOTS):
        mine[s : s + 1, :] = pulses[s]
    mbuf[pl.ds(pl.multiple_of(pm * RUN, RUN), RUN), :] = mine[...]

    row, col = iota((256, 256), 0), iota((256, 256), 1)
    hit = (row // 32 == col % 8) & (row % 32 == col // 8)
    perm[...] = jnp.where(hit, 1.0, 0.0).astype(BF16)

    low_half = iota((32, 128), 1) < LC

    def pack(group, k):
        lanes = y_lanes(k)
        rows = pl.ds(pl.multiple_of(group * 256, 256), 256)
        both = jnp.concatenate([x_ref[0, rows, lanes], x_ref[1, rows, lanes]], axis=1)
        turned = jnp.dot(perm[...], both, preferred_element_type=F32)
        at = pl.ds(pl.multiple_of(group * 32, 32), 32)
        for c in range(2):
            parts = [turned[32 * p : 32 * p + 32, 128 * c : 128 * c + 128] for p in range(RUN)]
            slots = []
            for s in range(SLOTS):
                total = parts[s] * coef[3 * s : 3 * s + 1, lanes]
                for d in (1, 2):
                    total = total + parts[s + d] * coef[3 * s + d : 3 * s + d + 1, lanes]
                slots.append(total)
            for j in range(CHUNKS):
                a, b = slots[j], slots[j + 3]
                first = jnp.where(low_half, a, pltpu.roll(b, LC, 1))
                second = jnp.where(low_half, pltpu.roll(a, LC, 1), b)
                prep[j, 2 * y_at(k), at, 128 * c : 128 * c + 128] = first.astype(BF16)
                prep[j, 2 * y_at(k) + 1, at, 128 * c : 128 * c + 128] = second.astype(BF16)
        return k

    my_rows = pl.ds(pl.multiple_of(em * LE, LE), LE)

    def samples(j, peer):
        return pltpu.make_async_remote_copy(
            src_ref=prep.at[j, peer],
            dst_ref=xbuf.at[j, my_rows],
            send_sem=xsend.at[j],
            recv_sem=xrecv.at[j],
            device_id=(peer, pm),
            device_id_type=pl.DeviceIdType.MESH,
        )

    def send_y(j, k):
        mate = 2 * y_at(k) + 1 - lax.rem(em, 2)
        samples(j, mate).start()
        if k:
            samples(j, 2 * y_at(k) + lax.rem(em, 2)).start()

    for i in range(NY):
        load(i).wait()
        lax.fori_loop(0, 4, pack, ORDER[i])
        if i == 0:
            pl.semaphore_wait(barrier, NE + NP - 2)
        send_y(0, ORDER[i])

    def send_samples(j):
        for k in ORDER:
            send_y(j, k)

    def send_slots(k, carry):
        pltpu.make_async_remote_copy(
            src_ref=mine,
            dst_ref=mbuf.at[pl.ds(pl.multiple_of(pm * RUN, RUN), RUN)],
            send_sem=msend,
            recv_sem=mrecv,
            device_id=(em, pulse_peer(k)),
            device_id_type=pl.DeviceIdType.MESH,
        ).start()
        return carry

    send_samples(1)
    lax.fori_loop(1, NP, send_slots, 0)
    send_samples(2)
    for j in range(CHUNKS):
        xbuf[j, my_rows, :] = prep[j, em]

    for copy in small[1:]:
        copy.wait()
    eye = iota((128, 128), 0) == iota((128, 128), 1)
    for i in range(BEAMS // 128):
        line = index_ref[0:1, 128 * i : 128 * i + 128].astype(F32)
        wanted = jnp.sum(jnp.where(eye, line, 0.0), axis=1, keepdims=True)
        choice = iota((128, sines_ref.shape[1]), 1).astype(F32) == wanted
        picked = jnp.sum(jnp.where(choice, sines_ref[...], 0.0), axis=1, keepdims=True)
        column[128 * i : 128 * i + 128, :] = jnp.broadcast_to(picked, (128, 128))

    factor = 1.0 / math.sqrt(E)

    def weigh(step, carry):
        rows = pl.ds(pl.multiple_of((step // 16) * 64, 64), 64)
        lanes = pl.ds(pl.multiple_of((step % 16) * 128, 128), 128)
        turns = pos_ref[0:1, lanes] * column[rows, :]
        cosine, sine = turn(turns - jnp.round(turns))
        real, imag = gain_ref[0:1, lanes] * factor, gain_ref[1:2, lanes] * factor
        wr[rows, lanes] = (real * cosine + imag * sine).astype(BF16)
        wi[rows, lanes] = (imag * cosine - real * sine).astype(BF16)
        return carry

    lax.fori_loop(0, 8 * 16, weigh, 0)

    def tabulate(step, carry):
        rows = pl.ds(pl.multiple_of(step * 32, 32), 32)
        p = iota((32, PULSES), 0) + step * 32
        product = jnp.bitwise_and(p * iota((32, PULSES), 1), PULSES - 1).astype(F32) / PULSES
        cosine, sine = turn(jnp.where(product < 0.5, product, product - 1.0))
        at = p.astype(F32) / (PULSES - 1)
        level, _ = turn(jnp.where(at < 0.5, at, at - 1.0))
        taper = (0.54 - 0.46 * level) / math.sqrt(PULSES)
        for i, value in enumerate((cosine * taper, sine * taper)):
            high = value.astype(BF16)
            tab[rows, 256 * i : 256 * i + 256] = high
            tab[rows, 512 + 256 * i : 512 + 256 * i + 256] = (value - high.astype(F32)).astype(BF16)
        return carry

    lax.fori_loop(0, PULSES // 32, tabulate, 0)

    def wait_bytes(ref, sem):
        pltpu.make_async_copy(ref, ref, sem).wait()

    wait_bytes(mbuf.at[pl.ds(0, RUN * (NP - 1))], mrecv)
    lane = iota((128, 128), 1)
    for k in range(2):
        for h in range(2):
            found = [mbuf[pl.ds(j + 3 * h, NP, stride=RUN), :] for j in range(CHUNKS)]
            found = jnp.concatenate(found + [jnp.zeros((NP, 128), F32)], axis=0)
            pulse = jnp.sum(jnp.where(lane == 2 * em + k, found, 0.0), axis=1, keepdims=True)
            row = iota((128, PULSES), 0)
            target = (RUN * (row % NP)).astype(F32) + pulse
            hit = (jnp.abs(iota((128, PULSES), 1).astype(F32) - target) < 0.5) & (row < 96)
            rows = jnp.dot(jnp.where(hit, 1.0, 0.0).astype(BF16), tab[...], preferred_element_type=F32)
            for part in range(2):
                cosine = rows[:, 512 * part : 512 * part + 256]
                sine = rows[:, 512 * part + 256 : 512 * part + 512]
                real = slice(128 * h, 128 * h + 128)
                imag = slice(256 + 128 * h, 256 + 128 * h + 128)
                tsel[k, part, real, 0:256] = cosine.astype(BF16)
                tsel[k, part, real, 256:512] = (-sine).astype(BF16)
                tsel[k, part, imag, 0:256] = sine.astype(BF16)
                tsel[k, part, imag, 256:512] = cosine.astype(BF16)

    my_beams = pl.ds(pl.multiple_of(pm * LB, LB), LB)
    for j in range(CHUNKS):
        wait_bytes(xbuf.at[j, pl.ds(0, LE * (NE - 1))], xrecv.at[j])

        def form(m, carry, j=j):
            rows = pl.ds(pl.multiple_of(m * 256, 256), 256)
            by_real = jnp.dot(wr[rows, :], xbuf[j], preferred_element_type=F32)
            by_imag = jnp.dot(wi[rows, :], xbuf[j], preferred_element_type=F32)
            beams[j, rows, 0:128] = (by_real[:, 0:128] - by_imag[:, 128:256]).astype(BF16)
            beams[j, rows, 128:256] = (by_real[:, 128:256] + by_imag[:, 0:128]).astype(BF16)
            return carry

        lax.fori_loop(0, 2, form, 0)

        def send_beams(k, carry, j=j):
            pltpu.make_async_remote_copy(
                src_ref=beams.at[j, pl.ds(pl.multiple_of(pulse_peer(k) * LB, LB), LB)],
                dst_ref=ybuf.at[j, my_beams],
                send_sem=bsend.at[j],
                recv_sem=brecv.at[j],
                device_id=(em, pulse_peer(k)),
                device_id_type=pl.DeviceIdType.MESH,
            ).start()
            return carry

        lax.fori_loop(1, NP, send_beams, 0)
        ybuf[j, my_beams, :] = beams[j, my_beams, :]

    for j in range(CHUNKS):
        wait_bytes(ybuf.at[j, pl.ds(0, LB * (NP - 1))], brecv.at[j])
        fbuf[0, 512 * j : 512 * j + 512, :] = ybuf[j, :, 0:128].astype(F32)
        fbuf[1, 512 * j : 512 * j + 512, :] = ybuf[j, :, 128:256].astype(F32)

    for b in range(LB):
        for c in range(2):
            got = [fbuf[c, pl.ds(512 * j + b, NP, stride=LB), :] for j in range(CHUNKS)]
            got = jnp.concatenate(got + [jnp.zeros((NP, 128), F32)], axis=0)
            flat = got.T.astype(BF16)
            for h in range(2):
                for k in range(2):
                    xt[k, 32 * b : 32 * b + 32, 256 * c + 128 * h : 256 * c + 128 * h + 128] = flat[
                        64 * h + 32 * k : 64 * h + 32 * k + 32
                    ]

    for k in range(2):
        for m in range(4):
            left = xt[k, 128 * m : 128 * m + 128, :]
            spec = jnp.dot(left, tsel[k, 0], preferred_element_type=F32)
            spec = spec + jnp.dot(left, tsel[k, 1], preferred_element_type=F32)
            power = spec[:, 0:256] * spec[:, 0:256] + spec[:, 256:512] * spec[:, 256:512]
            out_ref[4 * m : 4 * m + 4, 32 * k : 32 * k + 32, :] = power.reshape(4, 32, 256)

    wait_bytes(mbuf.at[pl.ds(0, RUN * (NP - 1))], msend)
    for j in range(CHUNKS):
        wait_bytes(xbuf.at[j, pl.ds(0, LE * (NE - 1))], xsend.at[j])
        wait_bytes(ybuf.at[j, pl.ds(0, LB * (NP - 1))], bsend.at[j])


def per_device(echoes, keep_mask, steer_index, element_position, element_gain, steer_sines):
    vmem = pl.BlockSpec(memory_space=pltpu.VMEM)
    dma = pltpu.SemaphoreType.DMA
    power = pl.pallas_call(
        kernel,
        out_shape=jax.ShapeDtypeStruct((LB, LC, PULSES), F32),
        in_specs=[pl.BlockSpec(memory_space=pltpu.HBM)] * 6,
        out_specs=vmem,
        scratch_shapes=[
            pltpu.VMEM((2, LE * RUN, CELLS), BF16),
            pltpu.VMEM(keep_mask.shape, I32),
            pltpu.VMEM((1, steer_index.shape[0]), I32),
            pltpu.VMEM((1, element_position.shape[0]), F32),
            pltpu.VMEM(element_gain.shape, F32),
            pltpu.VMEM((1, steer_sines.shape[0]), F32),
            pltpu.VMEM((CHUNKS, NE, LE, 256), BF16),
            pltpu.VMEM((CHUNKS, E, 256), BF16),
            pltpu.VMEM((BEAMS, E), BF16),
            pltpu.VMEM((BEAMS, E), BF16),
            pltpu.VMEM((CHUNKS, BEAMS, 256), BF16),
            pltpu.VMEM((CHUNKS, BEAMS, 256), BF16),
            pltpu.VMEM((2, CHUNKS * BEAMS, 128), F32),
            pltpu.VMEM((RUN, 128), F32),
            pltpu.VMEM((RUN * NP, 128), F32),
            pltpu.VMEM((3 * SLOTS, CELLS), F32),
            pltpu.VMEM((256, 256), BF16),
            pltpu.VMEM((PULSES, 1024), BF16),
            pltpu.VMEM((2, 2, 512, 512), BF16),
            pltpu.VMEM((2, 512, 512), BF16),
            pltpu.VMEM((BEAMS, 128), F32),
            dma((NY,)), dma((5,)), dma, dma, dma((CHUNKS,)), dma((CHUNKS,)), dma((CHUNKS,)), dma((CHUNKS,)),
        ],
        compiler_params=pltpu.CompilerParams(
            collective_id=0, has_side_effects=True, vmem_limit_bytes=63_000_000
        ),
        name="integrate",
    )(
        echoes.reshape(2, LE * RUN, CELLS),
        keep_mask,
        steer_index.reshape(1, -1),
        element_position.reshape(1, -1),
        element_gain,
        steer_sines.reshape(1, -1),
    )
    return jnp.transpose(power, (0, 2, 1))


def solution(mesh):
    placed = (P(None, "elem", "pulse", None), P("pulse", None), P(), P(), P(), P())
    return jax.shard_map(
        per_device, mesh=mesh, in_specs=placed, out_specs=P("pulse", None, "elem"), check_vma=False
    )
```

```python
import functools
import math

import jax
import jax.numpy as jnp
from jax import lax
from jax.experimental import pallas as pl
from jax.experimental.pallas import tpu as pltpu
from jax.sharding import PartitionSpec as P

F32 = jnp.float32
BF16 = jnp.bfloat16
I32 = jnp.int32
E = 2048
BEAMS = 512
PULSES = 256
CELLS = 1024
BLOCKS = 32
RUN = 8
SLOTS = 6
NE = 16
NP = 32
LE = E // NE
LB = BEAMS // NP
LC = CELLS // NE
CHUNKS = 3
NY = 8
UP, OWN, DOWN = 0, 7, 9
TILES = 12
HALF = BEAMS // 2
ORDER = (3, 5, 4, 2, 6, 1, 7, 0)


def turn(t):
    a = t * math.pi
    q = a * a
    s = a * (1.0 + q * (-1 / 6 + q * (1 / 120 + q * (-1 / 5040 + q * (1 / 362880 - q / 39916800)))))
    c = 1.0 + q * (-1 / 2 + q * (1 / 24 + q * (-1 / 720 + q * (1 / 40320 + q * (-1 / 3628800 + q / 479001600)))))
    return 1.0 - 2.0 * s * s, 2.0 * s * c


def iota(shape, dim):
    return lax.broadcasted_iota(I32, shape, dim)


def slot_pulses(keep):
    count = jnp.zeros_like(keep[0:1])
    first = jnp.zeros_like(count)
    second = jnp.zeros_like(count)
    for p in range(RUN):
        count = count + (1.0 - keep[p : p + 1])
        first = first + jnp.where(count < 0.5, 1.0, 0.0)
        second = second + jnp.where(count < 1.5, 1.0, 0.0)
    return [
        s + jnp.where(first < s + 0.5, 1.0, 0.0) + jnp.where(second < s + 1.5, 1.0, 0.0)
        for s in range(SLOTS)
    ]


def kernel(
    x_hbm, mask_hbm, index_hbm, pos_hbm, gain_hbm, sines_hbm, out_ref,
    x_ref, mask_ref, index_ref, pos_ref, gain_ref, sines_ref, prep, xbuf, wr, wi, psend, pbuf, own, beams, ybuf, fbuf, mine, mbuf, coef, perm, tab, tsel, xt, column,
    lsem, ssem, msend, mrecv, xsend, xrecv, ssum, rsum, bsend, brecv,
):
    em = lax.axis_index("elem")
    pm = lax.axis_index("pulse")
    barrier = pltpu.get_barrier_semaphore()

    small = [
        pltpu.make_async_copy(a, b, ssem.at[i])
        for i, (a, b) in enumerate((
            (mask_hbm, mask_ref), (index_hbm, index_ref), (pos_hbm, pos_ref), (gain_hbm, gain_ref), (sines_hbm, sines_ref)
        ))
    ]
    for copy in small:
        copy.start()

    def y_at(k):
        return lax.rem(em // 2 + k, NY)

    def y_lanes(k):
        return pl.ds(pl.multiple_of(y_at(k) * 128, 128), 128)

    def load(i):
        lanes = y_lanes(ORDER[i])
        return pltpu.make_async_copy(x_hbm.at[:, :, lanes], x_ref.at[:, :, lanes], lsem.at[i])

    for i in range(NY):
        load(i).start()
    def elem_peer(k):
        return lax.rem(em + k, NE)

    def pulse_peer(k):
        return lax.rem(pm + k, NP)

    def greet_elem(k, carry):
        pl.semaphore_signal(barrier, inc=1, device_id=(elem_peer(k), pm), device_id_type=pl.DeviceIdType.MESH)
        return carry

    def greet_pulse(k, carry):
        pl.semaphore_signal(barrier, inc=1, device_id=(em, pulse_peer(k)), device_id_type=pl.DeviceIdType.MESH)
        return carry

    lax.fori_loop(1, NE, greet_elem, 0)
    lax.fori_loop(1, NP, greet_pulse, 0)

    small[0].wait()
    keep = mask_ref[...].astype(F32)
    blocks_of = iota((BLOCKS, CELLS), 1) // (CELLS // BLOCKS) == iota((BLOCKS, CELLS), 0)
    keep_cells = jnp.dot(keep, jnp.where(blocks_of, 1.0, 0.0), preferred_element_type=F32)
    pulses = slot_pulses(keep_cells)
    for s in range(SLOTS):
        for d in range(3):
            use = jnp.where(jnp.abs(pulses[s] - (s + d)) < 0.5, 1.0, 0.0)
            coef[3 * s + d : 3 * s + d + 1, :] = use * keep_cells[s + d : s + d + 1]
    narrow = jnp.where(iota((BLOCKS, 128), 1) == iota((BLOCKS, 128), 0), 1.0, 0.0)
    pulses = slot_pulses(jnp.dot(keep, narrow, preferred_element_type=F32))
    mine[...] = jnp.zeros_like(mine)
    for s in range(SLOTS):
        mine[s : s + 1, :] = pulses[s]
    mbuf[pl.ds(pl.multiple_of(pm * RUN, RUN), RUN), :] = mine[...]

    row, col = iota((256, 256), 0), iota((256, 256), 1)
    hit = (row // 32 == col % 8) & (row % 32 == col // 8)
    perm[...] = jnp.where(hit, 1.0, 0.0).astype(BF16)

    low_half = iota((32, 128), 1) < LC

    def pack(group, k):
        lanes = y_lanes(k)
        rows = pl.ds(pl.multiple_of(group * 256, 256), 256)
        both = jnp.concatenate([x_ref[0, rows, lanes], x_ref[1, rows, lanes]], axis=1)
        turned = jnp.dot(perm[...], both, preferred_element_type=F32)
        at = pl.ds(pl.multiple_of(group * 32, 32), 32)
        for c in range(2):
            parts = [turned[32 * p : 32 * p + 32, 128 * c : 128 * c + 128] for p in range(RUN)]
            slots = []
            for s in range(SLOTS):
                total = parts[s] * coef[3 * s : 3 * s + 1, lanes]
                for d in (1, 2):
                    total = total + parts[s + d] * coef[3 * s + d : 3 * s + d + 1, lanes]
                slots.append(total)
            for j in range(CHUNKS):
                a, b = slots[j], slots[j + 3]
                first = jnp.where(low_half, a, pltpu.roll(b, LC, 1))
                second = jnp.where(low_half, pltpu.roll(a, LC, 1), b)
                prep[j, 2 * y_at(k), at, 128 * c : 128 * c + 128] = first.astype(BF16)
                prep[j, 2 * y_at(k) + 1, at, 128 * c : 128 * c + 128] = second.astype(BF16)
        return k

    half = lax.rem(em, 2)

    def place(k, mate):
        if k == 0:
            return 0, OWN + half
        if k == 4:
            return (5, DOWN + 6) if mate else (3, UP)
        if k < 4:
            return k - 1, UP + 7 - 2 * k + half
        return (k + 1) % NY, DOWN + 2 * (7 - k) + half

    def block_rows(block):
        return pl.ds(pl.multiple_of(block * LE, LE), LE)

    def send_y(j, k):
        for mate in (1, 0):
            k2, block = place(k, mate)
            side = 1 - half if mate else half
            source = prep.at[j, 2 * y_at(k) + side]
            if k2 or mate:
                pltpu.make_async_remote_copy(
                    src_ref=source,
                    dst_ref=xbuf.at[j, block_rows(block)],
                    send_sem=xsend.at[j],
                    recv_sem=xrecv.at[j],
                    device_id=(2 * y_at(k2) + side, pm),
                    device_id_type=pl.DeviceIdType.MESH,
                ).start()
            else:
                xbuf[j, block_rows(block), :] = prep[j, 2 * y_at(k) + side]

    def send_slots(k, carry):
        pltpu.make_async_remote_copy(
            src_ref=mine,
            dst_ref=mbuf.at[pl.ds(pl.multiple_of(pm * RUN, RUN), RUN)],
            send_sem=msend,
            recv_sem=mrecv,
            device_id=(em, pulse_peer(k)),
            device_id_type=pl.DeviceIdType.MESH,
        ).start()
        return carry

    for i in range(NY):
        load(i).wait()
        lax.fori_loop(0, 4, pack, ORDER[i])
        if i == 0:
            pl.semaphore_wait(barrier, NE + NP - 2)
        send_y(0, ORDER[i])
        if i == 0:
            lax.fori_loop(1, NP, send_slots, 0)
    for k in ORDER:
        send_y(1, k)

    for copy in small[1:]:
        copy.wait()
    row, col = iota((128, 256), 0), iota((128, 256), 1)
    for i in range(BEAMS // 128):
        here = col == (row // LB) * (2 * LB) + LB * (i // 2) + row % LB
        line = index_ref[0:1, 256 * (i % 2) : 256 * (i % 2) + 256].astype(F32)
        wanted = jnp.sum(jnp.where(here, line, 0.0), axis=1, keepdims=True)
        choice = iota((128, sines_ref.shape[1]), 1).astype(F32) == wanted
        picked = jnp.sum(jnp.where(choice, sines_ref[...], 0.0), axis=1, keepdims=True)
        column[128 * i : 128 * i + 128, :] = jnp.broadcast_to(picked, (128, 128))

    factor = 1.0 / math.sqrt(E)

    def weigh(step, carry):
        rows = pl.ds(pl.multiple_of((step % 8) * 64, 64), 64)
        tile = step // 8
        to = pl.ds(pl.multiple_of(tile * 128, 128), 128)
        middle = lax.rem(2 * y_at(0) + tile + 11, NE)
        last = 2 * y_at(3) + 1 - half
        source = jnp.where(tile == 0, 2 * y_at(5) + half, jnp.where(tile == TILES - 1, last, middle))
        lanes = pl.ds(pl.multiple_of(source * 128, 128), 128)
        turns = pos_ref[0:1, lanes] * column[rows, :]
        cosine, sine = turn(turns - jnp.round(turns))
        real, imag = gain_ref[0:1, lanes] * factor, gain_ref[1:2, lanes] * factor
        wr[rows, to] = (real * cosine + imag * sine).astype(BF16)
        wi[rows, to] = (imag * cosine - real * sine).astype(BF16)
        return carry

    lax.fori_loop(0, 8 * TILES, weigh, 0)

    def tabulate(step, carry):
        rows = pl.ds(pl.multiple_of(step * 32, 32), 32)
        p = iota((32, PULSES), 0) + step * 32
        product = jnp.bitwise_and(p * iota((32, PULSES), 1), PULSES - 1).astype(F32) / PULSES
        cosine, sine = turn(jnp.where(product < 0.5, product, product - 1.0))
        at = p.astype(F32) / (PULSES - 1)
        level, _ = turn(jnp.where(at < 0.5, at, at - 1.0))
        taper = (0.54 - 0.46 * level) / math.sqrt(PULSES)
        for i, value in enumerate((cosine * taper, sine * taper)):
            high = value.astype(BF16)
            tab[rows, 256 * i : 256 * i + 256] = high
            tab[rows, 512 + 256 * i : 512 + 256 * i + 256] = (value - high.astype(F32)).astype(BF16)
        return carry

    lax.fori_loop(0, PULSES // 32, tabulate, 0)

    def wait_bytes(ref, sem):
        pltpu.make_async_copy(ref, ref, sem).wait()

    def pick_tables():
        wait_bytes(mbuf.at[pl.ds(0, RUN * (NP - 1))], mrecv)
        lane = iota((128, 128), 1)
        for k in range(2):
            for h in range(2):
                found = [mbuf[pl.ds(j + 3 * h, NP, stride=RUN), :] for j in range(CHUNKS)]
                found = jnp.concatenate(found + [jnp.zeros((NP, 128), F32)], axis=0)
                pulse = jnp.sum(jnp.where(lane == 2 * em + k, found, 0.0), axis=1, keepdims=True)
                row = iota((128, PULSES), 0)
                target = (RUN * (row % NP)).astype(F32) + pulse
                hit = (jnp.abs(iota((128, PULSES), 1).astype(F32) - target) < 0.5) & (row < 96)
                rows = jnp.dot(jnp.where(hit, 1.0, 0.0).astype(BF16), tab[...], preferred_element_type=F32)
                for part in range(2):
                    cosine = rows[:, 512 * part : 512 * part + 256]
                    sine = rows[:, 512 * part + 256 : 512 * part + 512]
                    real = slice(128 * h, 128 * h + 128)
                    imag = slice(256 + 128 * h, 256 + 128 * h + 128)
                    tsel[k, part, real, 0:256] = cosine.astype(BF16)
                    tsel[k, part, real, 256:512] = (-sine).astype(BF16)
                    tsel[k, part, imag, 0:256] = sine.astype(BF16)
                    tsel[k, part, imag, 256:512] = cosine.astype(BF16)

    def product(rows, tile, block, count, j):
        weights = pl.ds(128 * tile, 128 * count)
        samples = xbuf[j, 128 * block : 128 * block + 128 * count, :]
        by_real = jnp.dot(wr[rows, weights], samples, preferred_element_type=F32)
        by_imag = jnp.dot(wi[rows, weights], samples, preferred_element_type=F32)
        real = by_real[:, 0:128] - by_imag[:, 128:256]
        return jnp.concatenate([real, by_real[:, 128:256] + by_imag[:, 0:128]], axis=1)

    def sum_for_neighbours(j):
        wait_bytes(xbuf.at[j, pl.ds(0, LE * 13)], xrecv.at[j])
        for m in range(2):
            rows = pl.ds(HALF * m, HALF)
            for way, tile, block, k in ((0, 0, UP, 1), (1, 5, DOWN, 7)):
                psend[j, way, rows, :] = product(rows, tile, block, 7, j).astype(BF16)
                pltpu.make_async_remote_copy(
                    src_ref=psend.at[j, way, rows],
                    dst_ref=pbuf.at[j, way, rows],
                    send_sem=ssum.at[j],
                    recv_sem=rsum.at[2 * j + m],
                    device_id=(2 * y_at(k) + half, pm),
                    device_id_type=pl.DeviceIdType.MESH,
                ).start()

    def sum_own(j):
        for m in range(2):
            rows = pl.ds(HALF * m, HALF)
            own[j, rows, :] = product(rows, 5, OWN, 2, j)

    core = lax.rem(pm, 2)
    my_beams = pl.ds(pl.multiple_of((core * (NP // 2) + pm // 2) * LB, LB), LB)
    my_place = pl.ds(pl.multiple_of(pm * LB, LB), LB)

    def beams_copy(j, m, k):
        chip = lax.rem(pm // 2 + k, NP // 2)
        return pltpu.make_async_remote_copy(
            src_ref=beams.at[j, pl.ds(pl.multiple_of((m * (NP // 2) + chip) * LB, LB), LB)],
            dst_ref=ybuf.at[j, my_place],
            send_sem=bsend.at[j],
            recv_sem=brecv.at[j],
            device_id=(em, 2 * chip + m),
            device_id_type=pl.DeviceIdType.MESH,
        )

    def finish_beams(j):
        for m in range(2):
            rows = pl.ds(HALF * m, HALF)
            wait_bytes(pbuf.at[j, :, rows], rsum.at[2 * j + m])
            total = own[j, rows, :] + pbuf[j, 0, rows, :].astype(F32) + pbuf[j, 1, rows, :].astype(F32)
            beams[j, rows, :] = total.astype(BF16)

            def one(k, carry, m=m):
                beams_copy(j, m, lax.rem(5 * k, NP // 2)).start()
                return carry

            lax.fori_loop(1, NP // 2, one, 0)

            @pl.when(core != m)
            def _(m=m):
                beams_copy(j, m, 0).start()

        ybuf[j, my_place, :] = beams[j, my_beams, :]

    sum_for_neighbours(0)
    for k in ORDER:
        send_y(2, k)
    sum_own(0)
    sum_for_neighbours(1)
    pick_tables()
    finish_beams(0)
    sum_own(1)
    sum_for_neighbours(2)
    finish_beams(1)
    sum_own(2)
    finish_beams(2)

    for j in range(CHUNKS):
        wait_bytes(ybuf.at[j, pl.ds(0, LB * (NP - 1))], brecv.at[j])
        fbuf[0, 512 * j : 512 * j + 512, :] = ybuf[j, :, 0:128].astype(F32)
        fbuf[1, 512 * j : 512 * j + 512, :] = ybuf[j, :, 128:256].astype(F32)

    for b in range(LB):
        for c in range(2):
            got = [fbuf[c, pl.ds(512 * j + b, NP, stride=LB), :] for j in range(CHUNKS)]
            got = jnp.concatenate(got + [jnp.zeros((NP, 128), F32)], axis=0)
            flat = got.T.astype(BF16)
            for h in range(2):
                for k in range(2):
                    xt[k, 32 * b : 32 * b + 32, 256 * c + 128 * h : 256 * c + 128 * h + 128] = flat[
                        64 * h + 32 * k : 64 * h + 32 * k + 32
                    ]

    for k in range(2):
        for m in range(4):
            left = xt[k, 128 * m : 128 * m + 128, :]
            spec = jnp.dot(left, tsel[k, 0], preferred_element_type=F32)
            spec = spec + jnp.dot(left, tsel[k, 1], preferred_element_type=F32)
            power = spec[:, 0:256] * spec[:, 0:256] + spec[:, 256:512] * spec[:, 256:512]
            out_ref[4 * m : 4 * m + 4, 32 * k : 32 * k + 32, :] = power.reshape(4, 32, 256)

    wait_bytes(mbuf.at[pl.ds(0, RUN * (NP - 1))], msend)
    for j in range(CHUNKS):
        wait_bytes(xbuf.at[j, pl.ds(0, LE * 13)], xsend.at[j])
        wait_bytes(psend.at[j], ssum.at[j])
        wait_bytes(ybuf.at[j, pl.ds(0, LB * (NP - 1))], bsend.at[j])


def per_device(echoes, keep_mask, steer_index, element_position, element_gain, steer_sines):
    vmem = pl.BlockSpec(memory_space=pltpu.VMEM)
    dma = pltpu.SemaphoreType.DMA
    power = pl.pallas_call(
        kernel,
        out_shape=jax.ShapeDtypeStruct((LB, LC, PULSES), F32),
        in_specs=[pl.BlockSpec(memory_space=pltpu.HBM)] * 6,
        out_specs=vmem,
        scratch_shapes=[
            pltpu.VMEM((2, LE * RUN, CELLS), BF16),
            pltpu.VMEM(keep_mask.shape, I32),
            pltpu.VMEM((1, steer_index.shape[0]), I32),
            pltpu.VMEM((1, element_position.shape[0]), F32),
            pltpu.VMEM(element_gain.shape, F32),
            pltpu.VMEM((1, steer_sines.shape[0]), F32),
            pltpu.VMEM((CHUNKS, NE, LE, 256), BF16),
            pltpu.VMEM((CHUNKS, E, 256), BF16),
            pltpu.VMEM((BEAMS, 128 * TILES), BF16),
            pltpu.VMEM((BEAMS, 128 * TILES), BF16),
            pltpu.VMEM((CHUNKS, 2, BEAMS, 256), BF16),
            pltpu.VMEM((CHUNKS, 2, BEAMS, 256), BF16),
            pltpu.VMEM((CHUNKS, BEAMS, 256), F32),
            pltpu.VMEM((CHUNKS, BEAMS, 256), BF16),
            pltpu.VMEM((CHUNKS, BEAMS, 256), BF16),
            pltpu.VMEM((2, CHUNKS * BEAMS, 128), F32),
            pltpu.VMEM((RUN, 128), F32),
            pltpu.VMEM((RUN * NP, 128), F32),
            pltpu.VMEM((3 * SLOTS, CELLS), F32),
            pltpu.VMEM((256, 256), BF16),
            pltpu.VMEM((PULSES, 1024), BF16),
            pltpu.VMEM((2, 2, 512, 512), BF16),
            pltpu.VMEM((2, 512, 512), BF16),
            pltpu.VMEM((BEAMS, 128), F32),
            dma((NY,)), dma((5,)), dma, dma, dma((CHUNKS,)), dma((CHUNKS,)), dma((CHUNKS,)), dma((2 * CHUNKS,)), dma((CHUNKS,)), dma((CHUNKS,)),
        ],
        compiler_params=pltpu.CompilerParams(
            collective_id=0, has_side_effects=True, vmem_limit_bytes=63_000_000
        ),
        name="integrate",
    )(
        echoes.reshape(2, LE * RUN, CELLS),
        keep_mask,
        steer_index.reshape(1, -1),
        element_position.reshape(1, -1),
        element_gain,
        steer_sines.reshape(1, -1),
    )
    return jnp.transpose(power, (0, 2, 1))


def solution(mesh):
    placed = (P(None, "elem", "pulse", None), P("pulse", None), P(), P(), P(), P())
    return jax.shard_map(
        per_device, mesh=mesh, in_specs=placed, out_specs=P("pulse", None, "elem"), check_vma=False
    )
```

```python
import functools
import math

import jax
import jax.numpy as jnp
from jax import lax
from jax.experimental import pallas as pl
from jax.experimental.pallas import tpu as pltpu
from jax.sharding import PartitionSpec as P

F32 = jnp.float32
BF16 = jnp.bfloat16
I32 = jnp.int32
E = 2048
BEAMS = 512
PULSES = 256
CELLS = 1024
BLOCKS = 32
RUN = 8
SLOTS = 6
NE = 16
NP = 32
LE = E // NE
LB = BEAMS // NP
LC = CELLS // NE
CHUNKS = SLOTS
AHEAD = 3
NY = 8
UP, OWN, DOWN = 0, 7, 9
TILES = 12
HALF = BEAMS // 2
ORDER = (3, 5, 4, 2, 6, 1, 7, 0)


def turn(t):
    a = t * math.pi
    q = a * a
    s = a * (1.0 + q * (-1 / 6 + q * (1 / 120 + q * (-1 / 5040 + q * (1 / 362880 - q / 39916800)))))
    c = 1.0 + q * (-1 / 2 + q * (1 / 24 + q * (-1 / 720 + q * (1 / 40320 + q * (-1 / 3628800 + q / 479001600)))))
    return 1.0 - 2.0 * s * s, 2.0 * s * c


def iota(shape, dim):
    return lax.broadcasted_iota(I32, shape, dim)


def slot_pulses(keep):
    count = jnp.zeros_like(keep[0:1])
    first = jnp.zeros_like(count)
    second = jnp.zeros_like(count)
    for p in range(RUN):
        count = count + (1.0 - keep[p : p + 1])
        first = first + jnp.where(count < 0.5, 1.0, 0.0)
        second = second + jnp.where(count < 1.5, 1.0, 0.0)
    return [
        s + jnp.where(first < s + 0.5, 1.0, 0.0) + jnp.where(second < s + 1.5, 1.0, 0.0)
        for s in range(SLOTS)
    ]


def kernel(
    x_hbm, mask_hbm, index_hbm, pos_hbm, gain_hbm, sines_hbm, out_ref,
    x_ref, mask_ref, index_ref, pos_ref, gain_ref, sines_ref, prep, xbuf, wr, wi, psend, pbuf, own, beams, ybuf, fbuf, mine, mbuf, coef, perm, tab, tsel, xt, column,
    lsem, ssem, msend, mrecv, xsend, xrecv, ssum, rsum, bsend, brecv,
):
    em = lax.axis_index("elem")
    pm = lax.axis_index("pulse")
    barrier = pltpu.get_barrier_semaphore()

    small = [
        pltpu.make_async_copy(a, b, ssem.at[i])
        for i, (a, b) in enumerate((
            (mask_hbm, mask_ref), (index_hbm, index_ref), (pos_hbm, pos_ref), (gain_hbm, gain_ref), (sines_hbm, sines_ref)
        ))
    ]
    for copy in small:
        copy.start()

    def y_at(k):
        return lax.rem(em // 2 + k, NY)

    def y_lanes(k):
        return pl.ds(pl.multiple_of(y_at(k) * 128, 128), 128)

    def load(i):
        lanes = y_lanes(ORDER[i])
        return pltpu.make_async_copy(x_hbm.at[:, :, lanes], x_ref.at[:, :, lanes], lsem.at[i])

    for i in range(NY):
        load(i).start()
    def elem_peer(k):
        return lax.rem(em + k, NE)

    def pulse_peer(k):
        return lax.rem(pm + k, NP)

    def greet_elem(k, carry):
        pl.semaphore_signal(barrier, inc=1, device_id=(elem_peer(k), pm), device_id_type=pl.DeviceIdType.MESH)
        return carry

    def greet_pulse(k, carry):
        pl.semaphore_signal(barrier, inc=1, device_id=(em, pulse_peer(k)), device_id_type=pl.DeviceIdType.MESH)
        return carry

    lax.fori_loop(1, NE, greet_elem, 0)
    lax.fori_loop(1, NP, greet_pulse, 0)

    small[0].wait()
    keep = mask_ref[...].astype(F32)
    blocks_of = iota((BLOCKS, CELLS), 1) // (CELLS // BLOCKS) == iota((BLOCKS, CELLS), 0)
    keep_cells = jnp.dot(keep, jnp.where(blocks_of, 1.0, 0.0), preferred_element_type=F32)
    pulses = slot_pulses(keep_cells)
    for s in range(SLOTS):
        for d in range(3):
            use = jnp.where(jnp.abs(pulses[s] - (s + d)) < 0.5, 1.0, 0.0)
            coef[3 * s + d : 3 * s + d + 1, :] = use * keep_cells[s + d : s + d + 1]
    narrow = jnp.where(iota((BLOCKS, 128), 1) == iota((BLOCKS, 128), 0), 1.0, 0.0)
    pulses = slot_pulses(jnp.dot(keep, narrow, preferred_element_type=F32))
    mine[...] = jnp.zeros_like(mine)
    for s in range(SLOTS):
        mine[s : s + 1, :] = pulses[s]
    mbuf[pl.ds(pl.multiple_of(pm * RUN, RUN), RUN), :] = mine[...]

    row, col = iota((256, 256), 0), iota((256, 256), 1)
    hit = (row // 32 == col % 8) & (row % 32 == col // 8)
    perm[...] = jnp.where(hit, 1.0, 0.0).astype(BF16)

    low_half = iota((32, 128), 1) < LC

    def pack(group, k):
        lanes = y_lanes(k)
        rows = pl.ds(pl.multiple_of(group * 256, 256), 256)
        both = jnp.concatenate([x_ref[0, rows, lanes], x_ref[1, rows, lanes]], axis=1)
        turned = jnp.dot(perm[...], both, preferred_element_type=F32)
        at = pl.ds(pl.multiple_of(group * 32, 32), 32)
        packed = []
        for c in range(2):
            parts = [turned[32 * p : 32 * p + 32, 128 * c : 128 * c + 128] for p in range(RUN)]
            slots = []
            for s in range(SLOTS):
                total = parts[s] * coef[3 * s : 3 * s + 1, lanes]
                for d in (1, 2):
                    total = total + parts[s + d] * coef[3 * s + d : 3 * s + d + 1, lanes]
                slots.append(total)
            packed.append(slots)
        for j in range(CHUNKS):
            a, b = packed[0][j], packed[1][j]
            first = jnp.where(low_half, a, pltpu.roll(b, LC, 1))
            second = jnp.where(low_half, pltpu.roll(a, LC, 1), b)
            prep[j, 2 * y_at(k), at, :] = first.astype(BF16)
            prep[j, 2 * y_at(k) + 1, at, :] = second.astype(BF16)
        return k

    half = lax.rem(em, 2)

    def place(k, mate):
        if k == 0:
            return 0, OWN + half
        if k == 4:
            return (5, DOWN + 6) if mate else (3, UP)
        if k < 4:
            return k - 1, UP + 7 - 2 * k + half
        return (k + 1) % NY, DOWN + 2 * (7 - k) + half

    def block_rows(block):
        return pl.ds(pl.multiple_of(block * LE, LE), LE)

    def send_y(j, k):
        for mate in (1, 0):
            k2, block = place(k, mate)
            side = 1 - half if mate else half
            source = prep.at[j, 2 * y_at(k) + side]
            if k2 or mate:
                pltpu.make_async_remote_copy(
                    src_ref=source,
                    dst_ref=xbuf.at[j, block_rows(block)],
                    send_sem=xsend.at[j],
                    recv_sem=xrecv.at[j],
                    device_id=(2 * y_at(k2) + side, pm),
                    device_id_type=pl.DeviceIdType.MESH,
                ).start()
            else:
                xbuf[j, block_rows(block), :] = prep[j, 2 * y_at(k) + side]

    def send_slots(k, carry):
        pltpu.make_async_remote_copy(
            src_ref=mine,
            dst_ref=mbuf.at[pl.ds(pl.multiple_of(pm * RUN, RUN), RUN)],
            send_sem=msend,
            recv_sem=mrecv,
            device_id=(em, pulse_peer(k)),
            device_id_type=pl.DeviceIdType.MESH,
        ).start()
        return carry

    for i in range(NY):
        load(i).wait()
        lax.fori_loop(0, 4, pack, ORDER[i])
        if i == 0:
            pl.semaphore_wait(barrier, NE + NP - 2)
        send_y(0, ORDER[i])
        if i == 0:
            lax.fori_loop(1, NP, send_slots, 0)

    def send_chunk(j, carry):
        for k in ORDER:
            send_y(j, k)
        return carry

    lax.fori_loop(1, AHEAD, send_chunk, 0)

    for copy in small[1:]:
        copy.wait()
    row, col = iota((128, 256), 0), iota((128, 256), 1)
    for i in range(BEAMS // 128):
        here = col == (row // LB) * (2 * LB) + LB * (i // 2) + row % LB
        line = index_ref[0:1, 256 * (i % 2) : 256 * (i % 2) + 256].astype(F32)
        wanted = jnp.sum(jnp.where(here, line, 0.0), axis=1, keepdims=True)
        choice = iota((128, sines_ref.shape[1]), 1).astype(F32) == wanted
        picked = jnp.sum(jnp.where(choice, sines_ref[...], 0.0), axis=1, keepdims=True)
        column[128 * i : 128 * i + 128, :] = jnp.broadcast_to(picked, (128, 128))

    factor = 1.0 / math.sqrt(E)

    def weigh(step, carry):
        rows = pl.ds(pl.multiple_of((step % 8) * 64, 64), 64)
        tile = step // 8
        to = pl.ds(pl.multiple_of(tile * 128, 128), 128)
        middle = lax.rem(2 * y_at(0) + tile + 11, NE)
        last = 2 * y_at(3) + 1 - half
        source = jnp.where(tile == 0, 2 * y_at(5) + half, jnp.where(tile == TILES - 1, last, middle))
        lanes = pl.ds(pl.multiple_of(source * 128, 128), 128)
        turns = pos_ref[0:1, lanes] * column[rows, :]
        cosine, sine = turn(turns - jnp.round(turns))
        real, imag = gain_ref[0:1, lanes] * factor, gain_ref[1:2, lanes] * factor
        wr[rows, to] = (real * cosine + imag * sine).astype(BF16)
        wi[rows, to] = (imag * cosine - real * sine).astype(BF16)
        return carry

    lax.fori_loop(0, 8 * TILES, weigh, 0)

    def tabulate(step, carry):
        rows = pl.ds(pl.multiple_of(step * 32, 32), 32)
        p = iota((32, PULSES), 0) + step * 32
        product = jnp.bitwise_and(p * iota((32, PULSES), 1), PULSES - 1).astype(F32) / PULSES
        cosine, sine = turn(jnp.where(product < 0.5, product, product - 1.0))
        at = p.astype(F32) / (PULSES - 1)
        level, _ = turn(jnp.where(at < 0.5, at, at - 1.0))
        taper = (0.54 - 0.46 * level) / math.sqrt(PULSES)
        for i, value in enumerate((cosine * taper, sine * taper)):
            high = value.astype(BF16)
            tab[rows, 256 * i : 256 * i + 256] = high
            tab[rows, 512 + 256 * i : 512 + 256 * i + 256] = (value - high.astype(F32)).astype(BF16)
        return carry

    lax.fori_loop(0, PULSES // 32, tabulate, 0)

    def wait_bytes(ref, sem):
        pltpu.make_async_copy(ref, ref, sem).wait()

    def pick_tables():
        wait_bytes(mbuf.at[pl.ds(0, RUN * (NP - 1))], mrecv)
        lane = iota((128, 128), 1)
        for k in range(2):
            for h in range(2):
                found = [mbuf[pl.ds(j + 3 * h, NP, stride=RUN), :] for j in range(3)]
                found = jnp.concatenate(found + [jnp.zeros((NP, 128), F32)], axis=0)
                pulse = jnp.sum(jnp.where(lane == 2 * em + k, found, 0.0), axis=1, keepdims=True)
                row = iota((128, PULSES), 0)
                target = (RUN * (row % NP)).astype(F32) + pulse
                hit = (jnp.abs(iota((128, PULSES), 1).astype(F32) - target) < 0.5) & (row < 96)
                rows = jnp.dot(jnp.where(hit, 1.0, 0.0).astype(BF16), tab[...], preferred_element_type=F32)
                for part in range(2):
                    cosine = rows[:, 512 * part : 512 * part + 256]
                    sine = rows[:, 512 * part + 256 : 512 * part + 512]
                    real = slice(128 * h, 128 * h + 128)
                    imag = slice(256 + 128 * h, 256 + 128 * h + 128)
                    tsel[k, part, real, 0:256] = cosine.astype(BF16)
                    tsel[k, part, real, 256:512] = (-sine).astype(BF16)
                    tsel[k, part, imag, 0:256] = sine.astype(BF16)
                    tsel[k, part, imag, 256:512] = cosine.astype(BF16)

    def product(rows, tile, block, count, j):
        weights = pl.ds(128 * tile, 128 * count)
        samples = xbuf[j, 128 * block : 128 * block + 128 * count, :]
        by_real = jnp.dot(wr[rows, weights], samples, preferred_element_type=F32)
        by_imag = jnp.dot(wi[rows, weights], samples, preferred_element_type=F32)
        crossed = pltpu.roll(by_imag, LC, 1)
        return by_real + jnp.where(iota(crossed.shape, 1) < LC, -crossed, crossed)

    def sum_for_neighbours(j):
        wait_bytes(xbuf.at[j, pl.ds(0, LE * 13)], xrecv.at[j])
        for m in range(2):
            rows = pl.ds(HALF * m, HALF)
            for way, tile, block, k in ((0, 0, UP, 1), (1, 5, DOWN, 7)):
                psend[j, way, rows, :] = product(rows, tile, block, 7, j).astype(BF16)
                pltpu.make_async_remote_copy(
                    src_ref=psend.at[j, way, rows],
                    dst_ref=pbuf.at[j, way, rows],
                    send_sem=ssum.at[j],
                    recv_sem=rsum.at[2 * j + m],
                    device_id=(2 * y_at(k) + half, pm),
                    device_id_type=pl.DeviceIdType.MESH,
                ).start()

    def sum_own(j):
        for m in range(2):
            rows = pl.ds(HALF * m, HALF)
            own[j, rows, :] = product(rows, 5, OWN, 2, j)

    core = lax.rem(pm, 2)
    my_beams = pl.ds(pl.multiple_of((core * (NP // 2) + pm // 2) * LB, LB), LB)
    my_place = pl.ds(pl.multiple_of(pm * LB, LB), LB)

    def beams_copy(j, m, k):
        chip = lax.rem(pm // 2 + k, NP // 2)
        return pltpu.make_async_remote_copy(
            src_ref=beams.at[j, pl.ds(pl.multiple_of((m * (NP // 2) + chip) * LB, LB), LB)],
            dst_ref=ybuf.at[j, my_place],
            send_sem=bsend.at[j],
            recv_sem=brecv.at[j],
            device_id=(em, 2 * chip + m),
            device_id_type=pl.DeviceIdType.MESH,
        )

    def finish_beams(j):
        for m in range(2):
            rows = pl.ds(HALF * m, HALF)
            wait_bytes(pbuf.at[j, :, rows], rsum.at[2 * j + m])
            total = own[j, rows, :] + pbuf[j, 0, rows, :].astype(F32) + pbuf[j, 1, rows, :].astype(F32)
            beams[j, rows, :] = total.astype(BF16)

            def one(k, carry, m=m):
                beams_copy(j, m, lax.rem(5 * k, NP // 2)).start()
                return carry

            lax.fori_loop(1, NP // 2, one, 0)

            @pl.when(core != m)
            def _(m=m):
                beams_copy(j, m, 0).start()

        ybuf[j, my_place, :] = beams[j, my_beams, :]

    pick_tables()

    def advance(j, carry):
        sum_for_neighbours(j)

        @pl.when(j < CHUNKS - AHEAD)
        def _():
            send_chunk(j + AHEAD, 0)

        @pl.when(j > 1)
        def _():
            finish_beams(j - 2)

        sum_own(j)
        return carry

    lax.fori_loop(0, CHUNKS, advance, 0)
    finish_beams(CHUNKS - 2)
    finish_beams(CHUNKS - 1)

    for h in range(2):
        for j in range(3 * h, 3 * h + 3):
            wait_bytes(ybuf.at[j, pl.ds(0, LB * (NP - 1))], brecv.at[j])
            fbuf[512 * j : 512 * j + 512, :] = ybuf[j].astype(F32)
        for b in range(LB):
            got = [fbuf[pl.ds(512 * (3 * h + j) + b, NP, stride=LB), :] for j in range(3)]
            got = jnp.concatenate(got + [jnp.zeros((NP, 128), F32)], axis=0)
            flat = got.T.astype(BF16)
            for c in range(2):
                for k in range(2):
                    xt[k, 32 * b : 32 * b + 32, 256 * c + 128 * h : 256 * c + 128 * h + 128] = flat[
                        64 * c + 32 * k : 64 * c + 32 * k + 32
                    ]

    for k in range(2):
        for m in range(4):
            left = xt[k, 128 * m : 128 * m + 128, :]
            spec = jnp.dot(left, tsel[k, 0], preferred_element_type=F32)
            spec = spec + jnp.dot(left, tsel[k, 1], preferred_element_type=F32)
            power = spec[:, 0:256] * spec[:, 0:256] + spec[:, 256:512] * spec[:, 256:512]
            out_ref[4 * m : 4 * m + 4, 32 * k : 32 * k + 32, :] = power.reshape(4, 32, 256)

    wait_bytes(mbuf.at[pl.ds(0, RUN * (NP - 1))], msend)
    for j in range(CHUNKS):
        wait_bytes(xbuf.at[j, pl.ds(0, LE * 13)], xsend.at[j])
        wait_bytes(psend.at[j], ssum.at[j])
        wait_bytes(ybuf.at[j, pl.ds(0, LB * (NP - 1))], bsend.at[j])


def per_device(echoes, keep_mask, steer_index, element_position, element_gain, steer_sines):
    vmem = pl.BlockSpec(memory_space=pltpu.VMEM)
    dma = pltpu.SemaphoreType.DMA
    power = pl.pallas_call(
        kernel,
        out_shape=jax.ShapeDtypeStruct((LB, LC, PULSES), F32),
        in_specs=[pl.BlockSpec(memory_space=pltpu.HBM)] * 6,
        out_specs=vmem,
        scratch_shapes=[
            pltpu.VMEM((2, LE * RUN, CELLS), BF16),
            pltpu.VMEM(keep_mask.shape, I32),
            pltpu.VMEM((1, steer_index.shape[0]), I32),
            pltpu.VMEM((1, element_position.shape[0]), F32),
            pltpu.VMEM(element_gain.shape, F32),
            pltpu.VMEM((1, steer_sines.shape[0]), F32),
            pltpu.VMEM((CHUNKS, NE, LE, 128), BF16),
            pltpu.VMEM((CHUNKS, E, 128), BF16),
            pltpu.VMEM((BEAMS, 128 * TILES), BF16),
            pltpu.VMEM((BEAMS, 128 * TILES), BF16),
            pltpu.VMEM((CHUNKS, 2, BEAMS, 128), BF16),
            pltpu.VMEM((CHUNKS, 2, BEAMS, 128), BF16),
            pltpu.VMEM((CHUNKS, BEAMS, 128), F32),
            pltpu.VMEM((CHUNKS, BEAMS, 128), BF16),
            pltpu.VMEM((CHUNKS, BEAMS, 128), BF16),
            pltpu.VMEM((CHUNKS * BEAMS, 128), F32),
            pltpu.VMEM((RUN, 128), F32),
            pltpu.VMEM((RUN * NP, 128), F32),
            pltpu.VMEM((3 * SLOTS, CELLS), F32),
            pltpu.VMEM((256, 256), BF16),
            pltpu.VMEM((PULSES, 1024), BF16),
            pltpu.VMEM((2, 2, 512, 512), BF16),
            pltpu.VMEM((2, 512, 512), BF16),
            pltpu.VMEM((BEAMS, 128), F32),
            dma((NY,)), dma((5,)), dma, dma, dma((CHUNKS,)), dma((CHUNKS,)), dma((CHUNKS,)), dma((2 * CHUNKS,)), dma((CHUNKS,)), dma((CHUNKS,)),
        ],
        compiler_params=pltpu.CompilerParams(
            collective_id=0, has_side_effects=True, vmem_limit_bytes=40 << 20
        ),
        name="integrate",
    )(
        *(
            pltpu.with_memory_space_constraint(value, pltpu.HBM)
            for value in (
                echoes.reshape(2, LE * RUN, CELLS),
                keep_mask,
                steer_index.reshape(1, -1),
                element_position.reshape(1, -1),
                element_gain,
                steer_sines.reshape(1, -1),
            )
        )
    )
    return jnp.transpose(power, (0, 2, 1))


def solution(mesh):
    placed = (P(None, "elem", "pulse", None), P("pulse", None), P(), P(), P(), P())
    return jax.shard_map(
        per_device, mesh=mesh, in_specs=placed, out_specs=P("pulse", None, "elem"), check_vma=False
    )
```
